512 devices in a mesh: sub: 64 (over x, y, core), grp: 8 (over z).
Axes of the slice: x: 4, y: 8, z: 8, core: 2. Of those that a mesh axis runs over, the one named last changes fastest.
Arguments:
- schur: bfloat16 [64, 8, 1536, 1536], P('sub', 'grp'), as said below
- dual_load: float32 [64, 8, 16, 1536], P('sub', 'grp'), may hold values from -6 to 6
- modes: float32 [64, 8, 6, 1536], P('sub', 'grp'), may hold values from -0.15625 to 0.15625
- diag_stiff: float32 [64, 8, 1536], P('sub', 'grp'), may hold values from 0.5 to 4
- coarse_inverse: float32 [3072, 3072], P(('sub', 'grp')), as said below
- rigid_loads: float32 [64, 8, 6, 16], P('sub', 'grp'), may hold values from -24 to 24
- face_index: int32 [64, 8, 1536], P('sub', 'grp'), may hold values from 0 to 1535, each once within a row
Outputs:
- multipliers: float32 [64, 8, 16, 1536], P('sub', 'grp')
- projected_residual: float32 [64, 8, 16, 1536], P('sub', 'grp')
- amplitudes: float32 [64, 8, 6, 16], P('sub', 'grp')
The draws below stay inside these ranges and needn't reach their ends.
Inputs may be any that keep to these rules, and one draw needn't show every extreme that they name: Each subdomain's schur is symmetric positive definite. coarse_inverse is symmetric positive definite. Each subdomain's face_index is a permutation of its 1536 dofs.
All inputs are finite; a program needn't handle non-finite values.
Results may differ from the reference program's by a relative error of at most 0.0034.
Values sent between devices are 32-bit elements; how exact they have to be, the bound alone decides.
A program may use at most 64 MiB of HBM per device.

```python
import math
import jax
import jax.numpy as jnp
from jax import lax

INTF = 1536
MODES = 6
NRHS = 16
ITERS = 1
FACE = 256
LAT_A = 64
LAT_B = 8
NC = 3072


def draw_schur(key, part):

    def single(index):
        sub_key = jax.random.fold_in(key, index)
        first_key, second_key = jax.random.split(sub_key)
        base = jax.random.uniform(first_key, (INTF, INTF), jnp.float32, -1.0, 1.0)
        symmetric = (base + base.T) * 0.5
        identity = jnp.eye(INTF, dtype=jnp.float32)
        coupled = identity + jnp.where(identity > 0.5, 0.0, symmetric * (0.9 / INTF))
        scales = jnp.exp(jax.random.uniform(second_key, (INTF,), jnp.float32, math.log(0.5), math.log(2.0)))
        return (coupled * scales[:, None] * scales[None, :]).astype(jnp.bfloat16)
    flat = lax.map(single, jnp.arange(LAT_A * LAT_B))
    return flat.reshape(LAT_A, LAT_B, INTF, INTF)


def draw_coarse_inverse(key, part):
    first_key, second_key, third_key = jax.random.split(jax.random.fold_in(key, 17), 3)
    position = jnp.arange(NC)
    owner = position // MODES
    first_pos = owner // LAT_B
    second_pos = owner % LAT_B
    distance = jnp.abs(first_pos[:, None] - first_pos[None, :]) + jnp.abs(second_pos[:, None] - second_pos[None, :])
    apart = position[:, None] != position[None, :]
    near = (distance <= 1) & apart
    base = jax.random.uniform(first_key, (NC, NC), jnp.float32, -1.0, 1.0)
    other = jax.random.uniform(second_key, (NC, NC), jnp.float32, -1.0, 1.0)
    near_part = jnp.where(near, 0.025 * (base + base.T) * 0.5, 0.0)
    far_part = jnp.where(apart, 0.2 / math.sqrt(NC) * (other + other.T) * 0.5, 0.0)
    diagonal = jnp.exp(jax.random.uniform(third_key, (NC,), jnp.float32, 0.0, math.log(3.0)))
    return near_part + far_part + jnp.diag(diagonal)


def levels(key, dims, shards, smallest, high):
    loudness = 1.0
    for dim, shards_of in shards:
        draws = jax.random.uniform(jax.random.fold_in(jax.random.fold_in(key, 6), dim), (shards_of,), jnp.float32, smallest / len(shards), high / len(shards))
        loudness = loudness * jnp.repeat(jnp.exp(draws), dims[dim] // shards_of).reshape((-1,) + (1,) * (len(dims) - 1 - dim))
    return loudness


def centred(stream_key, shape, scale, limit, cuts=(), kind=jnp.bfloat16):
    level = levels(stream_key, shape, cuts, -0.22, 0.18) if cuts else 1.0
    drawn = jax.random.normal(stream_key, shape, jnp.float32) * scale * level
    return jnp.minimum(jnp.maximum(drawn, -limit), limit).astype(kind)


def setup_inputs(seed: int = 0) -> dict:
    splits = jax.random.split(jax.random.key(seed), 8)
    return {
        "schur": draw_schur(jax.random.fold_in(splits[7], 71), 0),
        "dual_load": centred(splits[1], (LAT_A, LAT_B, NRHS, INTF), 1.0, 6.0, ((0, 64), (1, 8)), jnp.float32),
        "modes": centred(splits[2], (LAT_A, LAT_B, MODES, INTF), INTF ** -0.5, 0.15625, ((0, 64), (1, 8)), jnp.float32),
        "diag_stiff": jnp.clip(jnp.exp(math.log(4.0) - 2.0794415 * jax.random.uniform(splits[3], (LAT_A, LAT_B, INTF), jnp.float32) ** levels(splits[3], (LAT_A, LAT_B, INTF), ((0, 64), (1, 8)), -0.2, 0.2)), 0.5, 4.0),
        "coarse_inverse": draw_coarse_inverse(jax.random.fold_in(splits[7], 71), 0),
        "rigid_loads": centred(splits[5], (LAT_A, LAT_B, MODES, NRHS), 4.0, 24.0, ((0, 64), (1, 8)), jnp.float32),
        "face_index": jax.vmap(lambda own: jax.random.permutation(own, INTF))(jax.random.split(splits[6], LAT_A * LAT_B)).reshape((LAT_A, LAT_B, INTF)).astype(jnp.int32),
    }


def neighbours(values):
    faces = values.reshape(values.shape[:3] + (6, FACE))
    empty = jnp.zeros_like(faces[:, :, :, 0])
    first = jnp.concatenate([empty[:1], faces[:-1, :, :, 1]], axis=0)
    second = jnp.concatenate([faces[1:, :, :, 0], empty[:1]], axis=0)
    third = jnp.concatenate([empty[:, :1], faces[:, :-1, :, 3]], axis=1)
    fourth = jnp.concatenate([faces[:, 1:, :, 2], empty[:, :1]], axis=1)
    return jnp.stack([first, second, third, fourth, empty, empty], axis=3).reshape(values.shape)


def assemble(values):
    return values - neighbours(values)


def reference(schur, dual_load, modes, diag_stiff, coarse_inverse, rigid_loads, face_index):
    count = LAT_A * LAT_B

    def reorder(pair):
        matrix, order = pair
        return jnp.take(jnp.take(matrix, order, axis=0), order, axis=1)

    schur_face = lax.map(reorder, (schur.reshape(count, INTF, INTF), face_index.reshape(count, INTF)))
    index_rows = face_index[:, :, None, :]
    load = jnp.take_along_axis(dual_load, index_rows, axis=3)
    rigid_modes = jnp.take_along_axis(modes, index_rows, axis=3)
    stiffness = jnp.take_along_axis(diag_stiff, face_index, axis=2)[:, :, None, :]

    first_pos = jnp.arange(LAT_A)[:, None] + jnp.zeros((1, LAT_B), jnp.int32)
    second_pos = jnp.zeros((LAT_A, 1), jnp.int32) + jnp.arange(LAT_B)[None, :]
    flags = jnp.stack([first_pos > 0, first_pos < LAT_A - 1, second_pos > 0, second_pos < LAT_B - 1,
                       first_pos < 0, first_pos < 0], axis=-1)
    weights = jnp.repeat(jnp.where(flags, 0.5, 1.0).astype(jnp.float32), FACE, axis=-1)[:, :, None, :]

    def apply_schur(values):
        def single(pair):
            return jnp.dot(pair[0].astype(jnp.bfloat16), pair[1], preferred_element_type=jnp.float32)
        flat = values.reshape(count, values.shape[2], INTF)
        return lax.map(single, (flat, schur_face)).reshape(values.shape)

    def coarse(local_sums):
        flat = local_sums.reshape(NC, local_sums.shape[3])
        solved = jnp.dot(coarse_inverse, flat, precision=lax.Precision.HIGHEST, preferred_element_type=jnp.float32)
        return solved.reshape(local_sums.shape)

    def lift(amplitudes):
        return jnp.einsum("abmc,abmi->abci", amplitudes, rigid_modes, precision=lax.Precision.HIGHEST)

    def project(values):
        local_sums = jnp.einsum("abmi,abci->abmc", rigid_modes, values, precision=lax.Precision.HIGHEST)
        amplitudes = coarse(local_sums)
        return values - assemble(lift(amplitudes)), amplitudes

    def inner(left, right):
        return jnp.sum(weights * left * right, axis=(0, 1, 3))

    scaling = stiffness + neighbours(stiffness)
    multipliers = assemble(lift(coarse(rigid_loads)))
    residual = assemble(load - apply_schur(multipliers))
    projected, amplitudes = project(residual)
    norm_now = inner(projected, scaling * projected)
    direction, unused = project(scaling * projected)
    for step in range(ITERS):
        image = assemble(apply_schur(direction))
        curvature = inner(direction, image)
        step_size = (norm_now / curvature)[None, None, :, None]
        multipliers = multipliers + step_size * direction
        residual = residual - step_size * image
        projected, amplitudes = project(residual)
        if step + 1 < ITERS:
            norm_next = inner(projected, scaling * projected)
            searched, unused = project(scaling * projected)
            direction = searched + (norm_next / norm_now)[None, None, :, None] * direction
            norm_now = norm_next
    restore = jnp.argsort(face_index, axis=2)[:, :, None, :]
    return (jnp.take_along_axis(multipliers, restore, axis=3),
            jnp.take_along_axis(projected, restore, axis=3),
            amplitudes)
```

```python
import functools

import jax
import jax.numpy as jnp
from jax import lax
from jax.experimental import pallas as pl
from jax.experimental.pallas import tpu as pltpu
from jax.sharding import PartitionSpec as P

MESH = pl.DeviceIdType.MESH
F32 = jnp.float32
BF16 = jnp.bfloat16

INTF = 1536
FACE = 256
NC = 3072
NRHS = 16
MODES = 6
ROWS = 48


def dot(a, b):
    return lax.dot_general(a, b, (((1,), (0,)), ((), ())), preferred_element_type=F32)


def dot_nt(a, b):
    return lax.dot_general(a, b, (((1,), (1,)), ((), ())), preferred_element_type=F32)


def split(x):
    high = x.astype(BF16)
    return high, (x - high.astype(F32)).astype(BF16)


def split3(x):
    high = x.astype(BF16)
    rest = x - high.astype(F32)
    middle = rest.astype(BF16)
    return high, middle, (rest - middle.astype(F32)).astype(BF16)


def hops(k, n):
    return min(k, n - k)


def wrap(v, n):
    return jnp.where(v >= n, v - n, v)


def kernel(
    schur_hbm, load_ref, modes_ref, stiff_ref, coarse_ref, rigid_ref, order_ref,
    mult_ref, proj_ref, amp_ref,
    schur, onehot, permuted, small, small_slot, coarse_raw, coarse_hot, coarse_mat,
    lift_slot_mat, lift_dof_mat, modes_ext, face_static, gathered, sent, received, scaling,
    row_ref,
    schur_sem, g_send, g_recv, c_send, c_recv, f_send, f_recv, x_send, x_recv,
):
    sub = lax.axis_index("sub")
    b = lax.axis_index("grp")
    x = lax.div(sub, 16)
    y = lax.rem(lax.div(sub, 2), 8)
    core = lax.rem(sub, 2)
    tile = (x * 2 + core) * 8 + y

    def at(dx, dy, dz):
        return {"sub": (wrap(x + dx, 4) * 8 + wrap(y + dy, 8)) * 2 + core, "grp": wrap(b + dz, 8)}

    along_z = sorted([(0, 0, k) for k in range(1, 8)], key=lambda t: -hops(t[2], 8))
    along_xy = sorted(
        [(i, j, 0) for i in range(4) for j in range(8) if i or j],
        key=lambda t: -(hops(t[0], 4) + hops(t[1], 8)),
    )
    other_core = {"sub": sub + 1 - 2 * core, "grp": b}
    beside = [
        {"sub": wrap(sub + 63, 64), "grp": b},
        {"sub": wrap(sub + 1, 64), "grp": b},
        {"sub": sub, "grp": wrap(b + 7, 8)},
        {"sub": sub, "grp": wrap(b + 1, 8)},
    ]
    exists = [sub > 0, sub < 63, b > 0, b < 7]

    barrier = pltpu.get_barrier_semaphore()
    partners = [at(*t) for t in along_xy + along_z] + beside[:2]
    for partner in partners:
        pl.semaphore_signal(barrier, inc=1, device_id=partner, device_id_type=MESH)
    schur_copy = pltpu.make_async_copy(schur_hbm.at[0, 0], schur, schur_sem)
    schur_copy.start()

    def remote(src, dst, send, recv, device):
        pltpu.make_async_remote_copy(
            src_ref=src, dst_ref=dst, send_sem=send, recv_sem=recv,
            device_id=device, device_id_type=MESH,
        ).start()

    def wait(ref, sem):
        pltpu.make_async_copy(ref, ref, sem).wait()

    def own_row(g):
        return gathered.at[g, tile, pl.ds(b, 1)]

    def start_z(g, row):
        gathered[g, tile, pl.ds(b, 1)] = row
        for t in along_z:
            remote(own_row(g), own_row(g), g_send.at[g, 0], g_recv.at[g, 0], at(*t))

    def wait_z(g):
        wait(gathered.at[g, 0, pl.ds(0, 7)], g_recv.at[g, 0])

    def start_xy(g):
        column = gathered.at[g, tile]
        for t in along_xy:
            remote(column, column, g_send.at[g, 1], g_recv.at[g, 1], at(*t))

    def wait_xy(g):
        wait(gathered.at[g, pl.ds(0, 31)], g_recv.at[g, 1])

    def start_core(g):
        for i in range(4):
            part = gathered.at[g, pl.ds((2 * i + core) * 8, 8)]
            remote(part, part, g_send.at[g, 2], g_recv.at[g, 2], other_core)

    def wait_core(g):
        wait(gathered.at[g, pl.ds(0, 32)], g_recv.at[g, 2])

    def exchange(g):
        for f in range(4):
            remote(
                sent.at[g, :, pl.ds(f * FACE, FACE)], received.at[g, f ^ 1],
                x_send.at[g, f], x_recv.at[g, f ^ 1], beside[f],
            )
        for f in range(4):
            wait(received.at[g, f], x_recv.at[g, f])

    order = order_ref[...].reshape(1, INTF)

    def make_onehot(i, carry):
        rows = pl.ds(pl.multiple_of(i * 128, 128), 128)
        dofs = lax.broadcasted_iota(jnp.int32, (128, INTF), 0) + i * 128
        onehot[rows, :] = jnp.where(dofs == order, 1.0, 0.0).astype(BF16)
        return carry

    lax.fori_loop(0, INTF // 128, make_onehot, 0)
    small[...] = jnp.zeros_like(small)
    small[0:MODES, :] = modes_ref[0, 0]
    small[MODES : MODES + 1, :] = stiff_ref[0]
    small[8:24, :] = load_ref[0, 0]
    pieces = split3(jnp.concatenate([small[...], jnp.zeros((8, INTF), F32)], axis=0))
    stacked = dot(jnp.concatenate(pieces, axis=0), onehot[...])
    small_slot[...] = (stacked[0:32] + stacked[32:64] + stacked[64:96])[0:24]
    face_static[0] = small_slot[0:8, 0 : 4 * FACE]
    coarse_raw[0] = jnp.zeros((8, NC), F32)
    coarse_raw[5] = jnp.zeros((8, NC), F32)
    coarse_raw[0, 0:MODES] = coarse_ref[...]
    lanes = lax.broadcasted_iota(jnp.int32, (8, 128), 1)
    row_ref[...] = jnp.zeros_like(row_ref)
    row_ref[0:MODES, 0:NRHS] = rigid_ref[0, 0]
    rigid = row_ref[...]
    row = rigid[0:1]
    for m in range(1, MODES):
        row = row + pltpu.roll(rigid[m : m + 1], NRHS * m, 1)

    pl.semaphore_wait(barrier, len(partners))

    start_z(0, row)
    for f in range(4):
        remote(
            face_static.at[0, :, pl.ds(f * FACE, FACE)], face_static.at[1, :, pl.ds((f ^ 1) * FACE, FACE)],
            f_send.at[f], f_recv.at[f ^ 1], beside[f],
        )
    for f in range(4):
        remote(
            coarse_raw.at[0], coarse_raw.at[1 + (f ^ 1)],
            c_send.at[f], c_recv.at[f ^ 1], beside[f],
        )
    schur_copy.wait()

    def permute(i, carry):
        columns = pl.ds(pl.multiple_of(i * FACE, FACE), FACE)

        def part(j, inner):
            rows = pl.ds(pl.multiple_of(j * 512, 512), 512)
            permuted[rows, columns] = dot(schur[rows, :], onehot[:, columns]).astype(BF16)
            return inner

        return lax.fori_loop(0, 3, part, carry)

    lax.fori_loop(0, 2, permute, 0)
    wait_z(0)
    start_xy(0)

    for f in range(4):
        wait(face_static.at[1, :, pl.ds(f * FACE, FACE)], f_recv.at[f])
    modes_ext[...] = jnp.zeros_like(modes_ext)
    modes_ext[0:MODES, :] = small_slot[0:MODES, :]
    scaling[...] = small_slot[MODES : MODES + 1, :]
    for f in range(4):
        columns = slice(f * FACE, (f + 1) * FACE)
        arrived = jnp.where(exists[f], face_static[1, :, columns], 0.0)
        modes_ext[8 + 8 * f : 8 + 8 * f + MODES, columns] = -arrived[0:MODES]
        scaling[:, columns] = scaling[:, columns] + arrived[MODES : MODES + 1]
    ext_high, ext_low = split(modes_ext[...])
    lift_slot_mat[:, 0:INTF] = ext_high
    lift_slot_mat[:, INTF : 2 * INTF] = ext_low
    lift_dof_mat[:, 0:INTF] = dot_nt(ext_high, onehot[...]).astype(BF16)
    lift_dof_mat[:, INTF : 2 * INTF] = dot_nt(ext_low, onehot[...]).astype(BF16)

    out_pos = lax.broadcasted_iota(jnp.int32, (1, 768), 1)
    place = out_pos % 128
    source = (((place // 8) % 8 * 2 + place // 64) * 8 + place % 8) * MODES + out_pos // 128
    coarse_hot[...] = jnp.where(
        lax.broadcasted_iota(jnp.int32, (768, 768), 0) == source, 1.0, 0.0
    ).astype(BF16)
    for f in range(4):
        wait(coarse_raw.at[1 + f], c_recv.at[f])
    for k in range(4):
        chunk = coarse_raw[:, :, 768 * k : 768 * (k + 1)].reshape(ROWS, 768)
        sorted_rows = dot(jnp.concatenate(split(chunk), axis=0), coarse_hot[...]).astype(BF16)
        for part in range(2):
            for m in range(MODES):
                coarse_mat[
                    (part * MODES + m) * ROWS : (part * MODES + m + 1) * ROWS, 128 * k : 128 * (k + 1)
                ] = sorted_rows[part * ROWS : (part + 1) * ROWS, 128 * m : 128 * (m + 1)]

    lax.fori_loop(2, 4, permute, 0)
    wait_xy(0)
    start_core(0)
    lax.fori_loop(4, 6, permute, 0)
    wait_core(0)

    own_modes = small_slot[0:8, :]
    load = small_slot[8:24, :]
    groups = lax.broadcasted_iota(jnp.int32, (ROWS, 128), 1) // NRHS

    def coarse(g):
        everyone = gathered[g].reshape(512, 128)
        high, low = split(everyone)
        product = dot(coarse_mat[...], jnp.concatenate([high, low], axis=1))
        half = MODES * ROWS
        z = product[0:half, 0:128] + product[0:half, 128:256] + product[half:, 0:128]
        picked = jnp.zeros((ROWS, 128), F32)
        for m in range(MODES):
            picked = jnp.where(groups == m, z[m * ROWS : (m + 1) * ROWS], picked)
        total = jnp.sum(everyone, axis=0, keepdims=True)
        last = lax.broadcasted_iota(jnp.int32, (ROWS, 128), 0) == ROWS - 1
        picked = jnp.where(last, total, picked)
        turned = jnp.transpose(jnp.concatenate([picked, jnp.zeros((128 - ROWS, 128), F32)], axis=0))
        amplitudes = turned[0:NRHS]
        for m in range(1, MODES):
            amplitudes = amplitudes + turned[m * NRHS : (m + 1) * NRHS]
        return amplitudes[:, 0:ROWS], turned[6 * NRHS : 7 * NRHS, ROWS - 1 : ROWS]

    def lift(amplitudes, matrix):
        product = dot(jnp.concatenate(split(amplitudes), axis=0), matrix[...])
        return product[0:NRHS, 0:INTF] + product[0:NRHS, INTF:] + product[NRHS:, 0:INTF]

    case = lax.broadcasted_iota(jnp.int32, (NRHS, 128), 0)
    lane = lax.broadcasted_iota(jnp.int32, (NRHS, 128), 1)

    def rows_of(values, extra=None):
        spread = jnp.zeros((NRHS, 128), F32)
        for m in range(MODES):
            column = jnp.sum(values * own_modes[m : m + 1], axis=1, keepdims=True)
            spread = jnp.where(lane == m * NRHS + case, column, spread)
        if extra is not None:
            spread = jnp.where(lane == MODES * NRHS + case, extra, spread)
        return jnp.sum(spread, axis=0, keepdims=True)

    def to_dof(values):
        product = dot_nt(jnp.concatenate(split3(values), axis=0), onehot[...])
        return product[0:NRHS] + product[NRHS : 2 * NRHS] + product[2 * NRHS :]

    def subtract_beside(g, values):
        parts = [
            values[:, f * FACE : (f + 1) * FACE] - jnp.where(exists[f], received[g, f], 0.0)
            for f in range(4)
        ]
        return jnp.concatenate(parts + [values[:, 4 * FACE :]], axis=1)

    multipliers, unused = coarse(0)
    multipliers = lift(multipliers, lift_dof_mat)
    sent[0] = load - dot(multipliers.astype(BF16), permuted[...])
    exchange(0)
    residual = subtract_beside(0, sent[0])

    start_z(1, rows_of(residual))
    residual_dof = to_dof(residual)
    wait_z(1)
    start_xy(1)
    wait_xy(1)
    start_core(1)
    wait_core(1)
    amplitudes, unused = coarse(1)
    projected = residual - lift(amplitudes, lift_slot_mat)
    scaled = scaling[...] * projected
    weights = jnp.concatenate(
        [jnp.full((1, FACE), jnp.where(e, 0.5, 1.0), F32) for e in exists] + [jnp.full((1, 2 * FACE), 1.0, F32)],
        axis=1,
    )
    norm_part = jnp.sum(weights * projected * scaled, axis=1, keepdims=True)

    start_z(2, rows_of(scaled, norm_part))
    scaled_dof = to_dof(scaled)
    wait_z(2)
    start_xy(2)
    wait_xy(2)
    start_core(2)
    wait_core(2)
    direction_amplitudes, norm = coarse(2)
    direction_dof = scaled_dof - lift(direction_amplitudes, lift_dof_mat)
    image_local = dot(direction_dof.astype(BF16), permuted[...])
    sent[1] = image_local
    direction = scaled - lift(direction_amplitudes, lift_slot_mat)
    curvature_part = jnp.sum(direction * image_local, axis=1, keepdims=True)
    exchange(1)
    image = subtract_beside(1, sent[1])

    start_z(3, rows_of(image, curvature_part))
    image_dof = to_dof(image)
    wait_z(3)
    start_xy(3)
    wait_xy(3)
    start_core(3)
    wait_core(3)
    image_amplitudes, curvature = coarse(3)
    step = norm / curvature
    mult_ref[0, 0] = multipliers + step * direction_dof
    amplitudes = amplitudes - step * image_amplitudes
    proj_ref[0, 0] = residual_dof - step * image_dof - lift(amplitudes, lift_dof_mat)
    amp_ref[0, 0] = jnp.transpose(
        jnp.concatenate([amplitudes, jnp.zeros((NRHS, 128 - ROWS), F32)], axis=1)
    )[0:MODES, :]

    for g in range(4):
        wait(gathered.at[g, 0, pl.ds(0, 7)], g_send.at[g, 0])
        wait(gathered.at[g, pl.ds(0, 31)], g_send.at[g, 1])
        wait(gathered.at[g, pl.ds(0, 32)], g_send.at[g, 2])
    for f in range(4):
        wait(face_static.at[1, :, pl.ds(f * FACE, FACE)], f_send.at[f])
        wait(coarse_raw.at[1 + f], c_send.at[f])
        for g in range(2):
            wait(received.at[g, f], x_send.at[g, f])


def body(schur, dual_load, modes, diag_stiff, coarse_inverse, rigid_loads, face_index):
    vmem = pl.BlockSpec(memory_space=pltpu.VMEM)
    return pl.pallas_call(
        kernel,
        out_shape=(
            jax.ShapeDtypeStruct((1, 1, NRHS, INTF), F32),
            jax.ShapeDtypeStruct((1, 1, NRHS, INTF), F32),
            jax.ShapeDtypeStruct((1, 1, MODES, NRHS), F32),
        ),
        in_specs=[pl.BlockSpec(memory_space=pl.ANY)] + [vmem] * 6,
        out_specs=(vmem, vmem, vmem),
        scratch_shapes=[
            pltpu.VMEM((INTF, INTF), BF16),
            pltpu.VMEM((INTF, INTF), BF16),
            pltpu.VMEM((INTF, INTF), BF16),
            pltpu.VMEM((24, INTF), F32),
            pltpu.VMEM((24, INTF), F32),
            pltpu.VMEM((6, 8, NC), F32),
            pltpu.VMEM((768, 768), BF16),
            pltpu.VMEM((2 * MODES * ROWS, 512), BF16),
            pltpu.VMEM((ROWS, 2 * INTF), BF16),
            pltpu.VMEM((ROWS, 2 * INTF), BF16),
            pltpu.VMEM((ROWS, INTF), F32),
            pltpu.VMEM((2, 8, 4 * FACE), F32),
            pltpu.VMEM((4, 64, 8, 128), F32),
            pltpu.VMEM((2, NRHS, INTF), F32),
            pltpu.VMEM((2, 4, NRHS, FACE), F32),
            pltpu.VMEM((1, INTF), F32),
            pltpu.VMEM((8, 128), F32),
            pltpu.SemaphoreType.DMA,
            pltpu.SemaphoreType.DMA((4, 3)),
            pltpu.SemaphoreType.DMA((4, 3)),
            pltpu.SemaphoreType.DMA((4,)),
            pltpu.SemaphoreType.DMA((4,)),
            pltpu.SemaphoreType.DMA((4,)),
            pltpu.SemaphoreType.DMA((4,)),
            pltpu.SemaphoreType.DMA((2, 4)),
            pltpu.SemaphoreType.DMA((2, 4)),
        ],
        compiler_params=pltpu.CompilerParams(
            collective_id=0, has_side_effects=True, vmem_limit_bytes=48 * 2**20
        ),
    )(schur, dual_load, modes, diag_stiff, coarse_inverse, rigid_loads, face_index)


def solution(mesh):
    placed = (
        P("sub", "grp", None, None),
        P("sub", "grp", None, None),
        P("sub", "grp", None, None),
        P("sub", "grp", None),
        P(("sub", "grp"), None),
        P("sub", "grp", None, None),
        P("sub", "grp", None),
    )
    return jax.shard_map(
        body,
        mesh=mesh,
        in_specs=placed,
        out_specs=(
            P("sub", "grp", None, None),
            P("sub", "grp", None, None),
            P("sub", "grp", None, None),
        ),
        check_vma=False,
    )
```
